512 devices in a mesh: pulse: 128 (over x, z, core), pol: 4 (over y).
Axes of the slice: x: 4, y: 4, z: 16, core: 2. Of those that a mesh axis runs over, the one named last changes fastest.
Arguments:
- echoes: bfloat16 [2, 4, 2048, 8192], P(None, 'pol', 'pulse'), may hold values from -6 to 6
- interp_weights: bfloat16 [64, 128, 128], replicated, may hold values from -0.5 to 0.5
- band_starts: int32 [64], replicated, may hold values from 0 to 8064, as said below
- row_lo: int32 [2048], P('pulse'), may hold values from 0 to 2047
- row_len: int32 [2048], P('pulse'), may hold values from 4098 to 8192, as said below
- tile_owner: int32 [4, 128, 512, 1], P('pol', 'pulse'), may hold values from 0 to 127; in each aligned block of 512 rows (0 to 511, 512 to 1023, ..., all dimensions but the last counted through in order) at most 8 rows name the same one
Outputs:
- coherency_tiles: float32 [10, 4, 128, 1024], P(None, 'pol', 'pulse')
The draws below stay inside these ranges and needn't reach their ends.
Inputs may be any that keep to these rules, and one draw needn't show every extreme that they name: `band_starts`: Non-decreasing over the bands, the first 0 and the last 8064. row_lo + row_len never passes 8192. `tile_owner`: among the 512 tiles of one block (g, j), no owner is named more than 8 times.
All inputs are finite; a program needn't handle non-finite values.
Results may differ from the reference program's by a relative error of at most 0.0011.
Values may be sent and summed in bfloat16 or wider, within the bound.
A program may use at most 128 MiB of HBM per device.

```python
import math
import jax
import jax.numpy as jnp
import numpy as np
from jax import lax

RANGE = 8192
PULSES = 2048
AZIMUTH = 2048
WINDOW = 128
BLOCK = 128
BLOCKS = 64
LOOK = 8
BAND = 64
QUARTER = 512
TILES_DEV = 512
MOST = 8
SLOTS = 1024
N_PULSE = 128
N_POL = 4


def span_pair(key):
    edge_key, rest_key = jax.random.split(jax.random.fold_in(key, 11))
    quarter_range = RANGE // 4
    lower_edge = jax.random.randint(edge_key, (PULSES,), 0, quarter_range, dtype=jnp.int32)
    spare_bins = jax.random.randint(rest_key, (PULSES,), 0, quarter_range, dtype=jnp.int32)
    lower_edge = lower_edge.at[0].set(0).at[1].set(quarter_range - 1)
    spare_bins = spare_bins.at[0].set(0).at[1].set(quarter_range - 1)
    return (lower_edge, RANGE - lower_edge - spare_bins)


def draw_row_lo(key, part):
    return span_pair(key)[0]


def draw_row_len(key, part):
    return span_pair(key)[1]


def draw_band_starts(key, part):
    key = jax.random.fold_in(key, 3)
    block_ids = jnp.arange(BLOCKS, dtype=jnp.int32)
    even_start = block_ids * (RANGE - WINDOW) // (BLOCKS - 1)
    jitter = jax.random.randint(key, (BLOCKS,), 0, 16, dtype=jnp.int32)
    starts = jnp.where(block_ids == 0, 0, jnp.where(block_ids == BLOCKS - 1, RANGE - WINDOW, even_start - jitter))
    return jnp.maximum(starts, 0).astype(jnp.int32)


def block_levels(stream_key, extent, cuts, smallest, high):
    level = 1.0
    for axis_at, parts in cuts:
        heights = jax.random.uniform(jax.random.fold_in(jax.random.fold_in(stream_key, 6), axis_at), (parts,), jnp.float32, smallest / len(cuts), high / len(cuts))
        level = level * jnp.repeat(jnp.exp(heights), extent[axis_at] // parts).reshape((-1,) + (1,) * (len(extent) - 1 - axis_at))
    return level


def deal_out(stream_key, own, number, rows, number_of, top, most, slope):
    order = jax.random.permutation(stream_key, number_of)
    packed, ordinary = load_shares(number_of, rows * top, most, slope, True), load_shares(number_of, rows * top, most, slope, False)
    places = jnp.arange(number_of)

    def named(lengths, turn):
        used = int((lengths > 0).sum())
        fixed = max(1, used // 4)
        moved = fixed + (places - fixed + turn * (used - fixed)) % max(1, number_of - fixed)
        return jnp.zeros((number_of,), jnp.int32).at[order[jnp.where(places < fixed, places, moved)]].set(jnp.asarray(lengths, jnp.int32))

    lengths = jnp.where(number % 4 == 0, named(packed, number // 4), named(ordinary, number - number // 4 - 1))
    mixed = jax.random.permutation(jax.random.fold_in(own, 3), number_of)
    source_of, sink = mixed[0:number_of // 2 * 2:2], mixed[1:number_of // 2 * 2:2]
    room = jnp.minimum(lengths[source_of] - 1, most - lengths[sink]) // 2
    room = jnp.where((source_of == order[0]) | (sink == order[0]) | (lengths[sink] == 0), 0, jnp.maximum(room, 0))
    moved = jax.random.randint(jax.random.fold_in(own, 4), (number_of // 2,), 0, 1 << 20) % (room + 1)
    lengths = lengths.at[source_of].add(-moved).at[sink].add(moved)
    labels = jnp.searchsorted(jnp.cumsum(lengths), jnp.arange(rows * top), side="right").astype(jnp.int32)
    grid = labels.reshape(top, rows).T
    grid = grid[jax.random.permutation(jax.random.fold_in(own, 1), rows)]
    turn = jax.random.randint(jax.random.fold_in(own, 2), (rows, 1), 0, top)
    return jnp.take_along_axis(grid, (jnp.arange(top)[None, :] + turn) % top, axis=1)


def load_shares(count, total, reach, skew, full):
    loads = [(1 << 20) // math.isqrt(grade ** skew) + 1 for grade in range(1, count + 1)]
    largest = reach if full else min(reach, max(-(-total // count), total * loads[0] // sum(loads)))
    least = 1 if total - largest >= count - 1 else 0
    given, spare = [largest] + [least] * (count - 1), total - largest - least * (count - 1)
    while spare > 0:
        free = [i for i in range(1, count) if given[i] < largest] or [i for i in range(1, count) if given[i] < reach]
        whole, remaining = sum([loads[i] for i in free]), spare
        for i in free:
            extra = min(reach - given[i], max(1, remaining * loads[i] // whole), spare)
            given[i] = given[i] + extra
            spare = spare - extra
    return np.array(given)


def scatter_about(key, dims, deviation, most, pieces=(), kind=jnp.bfloat16):
    values = jax.random.normal(key, dims, jnp.float32) * deviation
    if len(pieces) > 0:
        values = block_levels(key, dims, pieces, -0.22, 0.18) * values
    return jnp.clip(values, min=-most, max=most).astype(kind)


def setup_inputs(seed: int = 0) -> dict:
    splits = jax.random.split(jax.random.key(seed), 7)
    echoes = scatter_about(splits[0], (2, 4, PULSES, RANGE), 1.0, 6.0, ((1, 4), (2, 128)))
    interp_weights = scatter_about(splits[1], (BLOCKS, WINDOW, BLOCK), WINDOW ** -0.5, 0.5)
    band_starts = draw_band_starts(jax.random.fold_in(splits[6], 71), 0)
    row_lo = draw_row_lo(jax.random.fold_in(splits[6], 71), 0)
    row_len = draw_row_len(jax.random.fold_in(splits[6], 71), 0)
    tile_owner_keys = jax.random.split(jax.random.fold_in(splits[5], 1), N_POL * N_PULSE * TILES_DEV // TILES_DEV)
    tile_owner_turns = jax.random.permutation(jax.random.fold_in(splits[5], 3), N_POL * N_PULSE * TILES_DEV // TILES_DEV)
    tile_owner = jax.vmap(lambda own, number: deal_out(jax.random.fold_in(splits[5], 2), own, number, TILES_DEV, N_PULSE, 1, MOST, 2))(tile_owner_keys, tile_owner_turns).reshape((N_POL, N_PULSE, TILES_DEV, 1))
    return dict(echoes=echoes, interp_weights=interp_weights, band_starts=band_starts, row_lo=row_lo, row_len=row_len, tile_owner=tile_owner)


ROOT_HALF = 1.0 / math.sqrt(2.0)
EPSILON = 1e-06

def twiddle(first_bin, bin_count, pulses, azimuth):
    az_index = jnp.arange(bin_count, dtype=jnp.int32) + first_bin
    wave_number = (az_index - azimuth // 2) % pulses
    phase_index = jnp.arange(pulses, dtype=jnp.int32)[:, None] * wave_number[None, :] % pulses
    angles = phase_index.astype(jnp.float32) * (2.0 * math.pi / pulses)
    factor = 1.0 / math.sqrt(pulses)
    return ((jnp.cos(angles) * factor).astype(jnp.bfloat16), (jnp.sin(angles) * factor).astype(jnp.bfloat16))

def pauli(images):
    channels = images.astype(jnp.float32)
    first_vec = (channels[0] + channels[3]) * ROOT_HALF
    second_vec = (channels[0] - channels[3]) * ROOT_HALF
    third_vec = (channels[1] + channels[2]) * ROOT_HALF
    return jnp.stack([first_vec, second_vec, third_vec], axis=0).astype(jnp.bfloat16)

def coherency(tile_data):
    values = tile_data.astype(jnp.float32)
    real_part = values[:, :, 0]
    imag_part = values[:, :, 1]

    def pair(row_comp, col_comp):
        same = lax.optimization_barrier(jnp.mean(real_part[:, row_comp] * real_part[:, col_comp] + imag_part[:, row_comp] * imag_part[:, col_comp], axis=-1))
        turned = lax.optimization_barrier(jnp.mean(imag_part[:, row_comp] * real_part[:, col_comp] - real_part[:, row_comp] * imag_part[:, col_comp], axis=-1))
        return (same, turned)
    power_one = pair(0, 0)[0]
    power_two = pair(1, 1)[0]
    power_three = pair(2, 2)[0]
    cross_ab = pair(0, 1)
    cross_ac = pair(0, 2)
    cross_bc = pair(1, 2)
    span_total = power_one + power_two + power_three
    scale_back = 1.0 / (span_total + EPSILON)
    entries = [power_one, power_two, power_three, cross_ab[0], cross_ab[1], cross_ac[0], cross_ac[1], cross_bc[0], cross_bc[1]]
    return jnp.stack([entry * scale_back for entry in entries] + [span_total], axis=1)

def reference(echoes, interp_weights, band_starts, row_lo, row_len, tile_owner):

    def one_band(block_index):
        start_bin = band_starts[block_index]
        window = lax.dynamic_slice_in_dim(echoes, start_bin, WINDOW, 3).astype(jnp.float32)
        weights = interp_weights[block_index].astype(jnp.float32)
        values = jnp.einsum('cqpj,jk->cqkp', window, weights)
        range_bins = block_index * BLOCK + jnp.arange(BLOCK, dtype=jnp.int32)
        inside = (range_bins[:, None] >= row_lo[None, :]) & (range_bins[:, None] < (row_lo + row_len)[None, :])
        return jnp.where(inside, values, 0.0).astype(jnp.bfloat16)
    banded = lax.map(one_band, jnp.arange(BLOCKS, dtype=jnp.int32))
    annulus = banded.transpose(1, 2, 0, 3, 4).reshape(2, 4, RANGE, PULSES)
    cosine, sine_table = twiddle(0, AZIMUTH, PULSES, AZIMUTH)
    cosine = cosine.astype(jnp.float32)
    sine_table = sine_table.astype(jnp.float32)
    groups = annulus.reshape(2, 4, RANGE // 512, 512, PULSES).transpose(2, 0, 1, 3, 4)

    def one_group(group):
        samples = group.astype(jnp.float32)
        direct = jnp.einsum('cqmp,pa->cqma', samples, cosine)
        crossed = jnp.einsum('cqmp,pa->cqma', samples, sine_table)
        real_part = direct[0] + crossed[1]
        imag_part = direct[1] - crossed[0]
        return jnp.stack([real_part, imag_part], axis=0).astype(jnp.bfloat16)
    formed = lax.map(one_group, groups)
    images = formed.transpose(2, 1, 0, 3, 4).reshape(4, 2, RANGE, AZIMUTH)
    vectors = pauli(images)
    band_tiles = BAND // LOOK
    quarter_tiles = QUARTER // LOOK
    tile_data = vectors.reshape(3, 2, N_PULSE, band_tiles, LOOK, N_POL, quarter_tiles, LOOK)
    tile_data = tile_data.transpose(5, 2, 3, 6, 0, 1, 4, 7).reshape(N_POL * N_PULSE * TILES_DEV, 3, 2, LOOK * LOOK)
    values = coherency(tile_data).reshape(N_POL, N_PULSE, TILES_DEV, 10).transpose(3, 0, 1, 2)
    owners = tile_owner[..., 0]
    onehot = (owners[..., None] == jnp.arange(N_PULSE, dtype=jnp.int32)).astype(jnp.int32)
    running = jnp.cumsum(onehot, axis=2)
    slot_index = lax.optimization_barrier(jnp.sum(onehot * (running - 1), axis=-1))
    pol_ids = jnp.arange(N_POL, dtype=jnp.int32)[:, None, None]
    band_ids = jnp.arange(N_PULSE, dtype=jnp.int32)[None, :, None]
    target = band_ids * MOST + slot_index
    result = jnp.zeros((10, N_POL, N_PULSE, SLOTS), jnp.float32)
    return result.at[:, pol_ids, owners, target].set(values)
```

```python
import math

import jax
import jax.numpy as jnp
import ml_dtypes
import numpy as np
from jax import lax
from jax.experimental import pallas as pl
from jax.experimental.pallas import tpu as pltpu
from jax.sharding import PartitionSpec as P

MESH = pl.DeviceIdType.MESH
ROOT_HALF = 1.0 / math.sqrt(2.0)
EPSILON = 1e-06
F32 = jnp.float32
BF16 = jnp.bfloat16

NX, NY, NZ, NC = 4, 4, 16, 2
PLANE = NX * NY * NC
GROUP = NX * NC
PULSES = 2048
ROWS = 1024
OWNERS = 128
TILES = 512
STEP = 16


def tables():
    row = np.arange(ROWS)
    azimuth = (row // 64 * 8 + row % 8) * 8 + row % 64 // 8
    z = np.arange(NZ)[:, None]
    k = np.arange(128)[None, :]
    pulse = (k // 32) * 512 + z * 32 + (k // 16 % 2) * 16 + k % 16
    m = azimuth[None, :, None] * pulse[:, None, :] % PULSES
    angles = m.astype(np.float32) * np.float32(2.0 * math.pi / PULSES)
    factor = np.float32(1.0 / math.sqrt(PULSES))
    both = np.concatenate([np.cos(angles) * factor, np.sin(angles) * factor], axis=2)
    return both.astype(ml_dtypes.bfloat16)


def selectors():
    sel = np.zeros((2, 16, 5, 2, 2, 4, 8), np.float32)
    for turn in range(2):
        for v in range(3):
            sel[turn, v, 0, :, turn, v] = 1
            sel[turn, 9, 0, :, turn, v] = 1
        for v, same, crossed, first in ((3, 1, 3, 0), (5, 2, 4, 0), (7, 1, 3, 1)):
            sel[turn, v, same, :, turn, first] = 1
            sel[turn, v + 1, crossed, 1, turn, first] = 1
            sel[turn, v + 1, crossed, 0, turn, first] = -1
    sel = sel.reshape(32, 640) / 64.0
    before = np.triu(np.ones((TILES, TILES), np.float32), 1)
    lanes = np.arange(128)
    spread = (np.arange(16)[:, None] == lanes[None, :] // 8) & (np.arange(16)[:, None] < 10)
    pick = np.concatenate([lanes[:, None] == v * 8 + lanes[None, :] % 8 for v in range(10)], axis=1)
    return [a.astype(ml_dtypes.bfloat16) for a in (sel, before, spread, pick)]


def split3(value):
    high = value.astype(BF16)
    rest = value - high.astype(F32)
    mid = rest.astype(BF16)
    low = (rest - mid.astype(F32)).astype(BF16)
    return high, mid, low


def swap_pieces(tiles, widths):
    lane = lax.broadcasted_iota(jnp.int32, (16, 128), 1) // 8
    tiles = list(tiles)
    for w in widths:
        upper = (lane & w) != 0
        for i in range(len(tiles)):
            if i & w:
                continue
            a, b = tiles[i], tiles[i | w]
            if a is None and b is None:
                continue
            a_down = 0.0 if a is None else pltpu.roll(a, 128 - 8 * w, 1)
            b_up = 0.0 if b is None else pltpu.roll(b, 8 * w, 1)
            tiles[i] = jnp.where(upper, b_up, 0.0 if a is None else a)
            tiles[i | w] = jnp.where(upper, 0.0 if b is None else b, a_down)
    return tiles


def resample_body(starts, lo, length, echo, weights, out):
    row = lax.broadcasted_iota(jnp.int32, (16, 128), 0)
    lane = lax.broadcasted_iota(jnp.int32, (16, 128), 1)
    lane2 = lax.broadcasted_iota(jnp.int32, (32, 128), 1)
    first = jnp.zeros((16, 128), jnp.int32)
    last = jnp.zeros((16, 128), jnp.int32)
    for r in range(16):
        first = jnp.where(row == r, lo[r], first)
        last = jnp.where(row == r, lo[r] + length[r], last)
    for n in range(STEP):
        band = pl.program_id(0) * STEP + n
        start = starts[band]
        base = jnp.minimum(start // 128, 62) * 128
        shift = start - base
        window = echo[:, :, pl.ds(pl.multiple_of(base, 128), 256)].astype(F32).reshape(32, 256)
        turn = (128 - shift) % 128
        left = pltpu.roll(window[:, :128], turn, 1)
        right = pltpu.roll(window[:, 128:], turn, 1)
        samples = jnp.where(lane2 < 128 - shift, left, right).astype(BF16)
        values = jnp.dot(samples, weights[n], preferred_element_type=F32).reshape(2, 16, 128)
        bins = band * 128 + lane
        inside = (bins >= first) & (bins < last)
        out[n] = jnp.where(inside[None], values, 0.0).astype(BF16)


def resample(echo, weights, starts, lo, length):
    smem = pl.BlockSpec(memory_space=pltpu.SMEM)
    return pl.pallas_call(
        resample_body,
        grid=(64 // STEP,),
        out_shape=jax.ShapeDtypeStruct((64, 2, 16, 128), BF16),
        in_specs=[
            smem,
            smem,
            smem,
            pl.BlockSpec((2, 16, 8192), lambda n: (0, 0, 0)),
            pl.BlockSpec((STEP, 128, 128), lambda n: (n, 0, 0)),
        ],
        out_specs=pl.BlockSpec((STEP, 2, 16, 128), lambda n: (n, 0, 0, 0)),
        compiler_params=pltpu.CompilerParams(vmem_limit_bytes=16 * 1024 * 1024),
    )(starts, lo, length, echo, weights)


def body(
    snd, owner, table, sel, before, spread, pick,
    out,
    tv, prcv, zsnd, zrcv, acc, sums, vout, grcv, onehot, slotmask, fsnd, frcv,
    load_sem, psend, precv, zsend, zrecv, gsend, grecv, fsend, frecv,
):
    pulse = lax.axis_index("pulse")
    y = lax.axis_index("pol")
    x, z, core = pulse // 32, pulse // 2 % 16, pulse % 2
    rank = x * 8 + y * 2 + core

    def plane_peer(k):
        px, py, pc = (x + k // 8) % 4, (y + k // 2 % 4) % 4, (core + k) % 2
        return ((px * 16 + z) * 2 + pc, py), px * 8 + py * 2 + pc

    def z_peer(k):
        pz = (z + k) % 16
        return ((x * 16 + pz) * 2 + core, y), pz

    load_t = pltpu.make_async_copy(table, tv, load_sem)
    load_t.start()

    barrier = pltpu.get_barrier_semaphore()

    @pl.loop(1, PLANE)
    def _(k):
        pl.semaphore_signal(barrier, inc=1, device_id=plane_peer(k)[0], device_id_type=MESH)

    @pl.loop(1, NZ)
    def _(k):
        pl.semaphore_signal(barrier, inc=1, device_id=z_peer(k)[0], device_id_type=MESH)

    row16 = lax.broadcasted_iota(jnp.int32, (16, 128), 0)
    lane16 = lax.broadcasted_iota(jnp.int32, (16, 128), 1)

    def plane_send(h):
        @pl.loop(1, PLANE)
        def _(k):
            device, to = plane_peer(k)
            pltpu.make_async_remote_copy(
                snd.at[2 * to + h], prcv.at[h, rank], psend.at[h], precv.at[h], device_id=device, device_id_type=MESH
            ).start()

        pltpu.make_async_copy(snd.at[2 * rank + h], prcv.at[h, rank], precv.at[h]).start()

    def plane_all(h, count):
        return pltpu.make_async_remote_copy(
            prcv.at[h, pl.ds(0, count)], prcv.at[h, pl.ds(0, count)], psend.at[h], precv.at[h],
            device_id=plane_peer(1)[0], device_id_type=MESH,
        )

    pl.semaphore_wait(barrier, PLANE - 1 + NZ - 1)
    plane_send(0)
    plane_send(1)

    def pack(h):
        plane_all(h, PLANE).wait_recv()
        for t in range(3):
            tiles = []
            for part in range(2):
                for g in range(GROUP):
                    def channel(q):
                        return prcv[h, g // 2 * 8 + q * 2 + g % 2, part].astype(F32)

                    if t == 0:
                        value = channel(0) + channel(3)
                    elif t == 1:
                        value = channel(0) - channel(3)
                    else:
                        value = channel(1) + channel(2)
                    tiles.append(value * ROOT_HALF)
            for to, tile in enumerate(swap_pieces(tiles, (1, 2, 4, 8))):
                zsnd[h, to, t] = tile.astype(BF16)

        @pl.loop(1, NZ)
        def _(k):
            device, to = z_peer(k)
            pltpu.make_async_remote_copy(
                zsnd.at[h, to], zrcv.at[h, z], zsend.at[h], zrecv.at[h, z], device_id=device, device_id_type=MESH
            ).start()

        zrcv[h, z] = zsnd[h, z]

    pack(0)
    pack(1)

    names = owner[...] == lax.broadcasted_iota(jnp.int32, (OWNERS, TILES), 0)
    mine = jnp.where(names, 1.0, 0.0).astype(BF16)
    onehot[...] = mine
    earlier = jnp.dot(mine, before[...], preferred_element_type=F32)
    earlier = jnp.where(names, earlier, 0.0).astype(BF16)
    slot = lax.dot_general(
        earlier, jnp.ones((OWNERS, 128), BF16), (((0,), (0,)), ((), ())), preferred_element_type=F32
    )
    lane_slot = (lax.broadcasted_iota(jnp.int32, (TILES, 128), 1) % 8).astype(F32)
    slotmask[...] = jnp.where(slot == lane_slot, 1.0, 0.0)
    load_t.wait()

    sign_row = (1 - 2 * (row16 % 2)).astype(F32)
    sign_part = jnp.where(lane16 < 64, 1.0, -1.0)

    def accumulate(h, source):
        tiles = [zrcv[h, source, t].astype(F32) for t in range(3)] + [None] * 5
        plain, turned = [], []
        for tile in swap_pieces(tiles, (1, 2, 4)):
            tile = tile + pltpu.roll(tile, 32, 1) * sign_row
            plain.append(tile.astype(BF16))
            turned.append((pltpu.roll(tile, 64, 1) * sign_part).astype(BF16))
        samples = jnp.concatenate(plain + turned, axis=0)
        return jnp.dot(tv[source], samples, preferred_element_type=F32)

    def form(h):
        acc[...] = accumulate(h, z)

        @pl.loop(1, NZ)
        def _(k):
            step = (k + 1) // 2
            source = (z + jnp.where(k % 2 == 1, step, 16 - step)) % 16
            pltpu.make_async_remote_copy(
                zsnd.at[h, 0], zrcv.at[h, source], zsend.at[h], zrecv.at[h, source],
                device_id=z_peer(1)[0], device_id_type=MESH,
            ).wait_recv()
            acc[...] += accumulate(h, source)

        @pl.loop(0, ROWS // 64)
        def _(k):
            a = acc[pl.ds(pl.multiple_of(k * 64, 64), 64), :]
            b1 = pltpu.roll(a, 120, 1)
            b2 = pltpu.roll(a, 112, 1)
            others = (a, b1, b2, pltpu.roll(b1, 64, 1), pltpu.roll(b2, 64, 1))
            for n, other in enumerate(others):
                sums[pl.ds(pl.multiple_of(k * 8, 8), 8), n * 128 : (n + 1) * 128] = jnp.sum(
                    (a * other).reshape(8, 8, 128), axis=0
                )

        entries = sum(
            lax.dot_general(sel[...], part, (((1,), (1,)), ((), ())), preferred_element_type=F32)
            for part in split3(sums[...])
        )
        for turn in range(2):
            entry = entries[turn * 16 : turn * 16 + 16]
            span = entry[9:10]
            scale = 1.0 / (span + EPSILON)
            vout[h, turn] = jnp.where(lax.broadcasted_iota(jnp.int32, (16, 128), 0) == 9, entry, entry * scale)

    def gather(h, action):
        for g in range(NY):
            device = (x * 32 + (y * 4 + core * 2 + h) * 2 + z // 8, jnp.int32(g))
            here = (device[0] == pulse) & (y == g)
            source, target = vout.at[h, 1 - g // 2], grcv.at[z % 8]

            @pl.when(jnp.logical_not(here))
            def _():
                copy = pltpu.make_async_remote_copy(
                    source, target, gsend, grecv, device_id=device, device_id_type=MESH
                )
                if action == "start":
                    copy.start()
                else:
                    copy.wait_send()

            if action == "start":

                @pl.when(here)
                def _():
                    pltpu.make_async_copy(source, target, grecv).start()

    for h in range(2):
        form(h)
        gather(h, "start")

    pltpu.make_async_remote_copy(grcv, grcv, gsend, grecv, device_id=plane_peer(1)[0], device_id_type=MESH).wait_recv()
    chunks = []
    odd = (y % 2) == 1
    for n in range(4):
        even_row, odd_row = grcv[2 * n], grcv[2 * n + 1]
        low = jnp.where(lane16 < 64, even_row, pltpu.roll(odd_row, 64, 1))
        high = jnp.where(lane16 < 64, pltpu.roll(even_row, 64, 1), odd_row)
        chunks.append(jnp.where(odd, high, low))
    values = jnp.concatenate(chunks, axis=1)
    wide = sum(
        lax.dot_general(part, spread[...], (((0,), (0,)), ((), ())), preferred_element_type=F32)
        for part in split3(values)
    )
    dealt = sum(
        jnp.dot(onehot[...], part, preferred_element_type=F32) for part in split3(wide * slotmask[...])
    )
    fsnd[...] = dealt.reshape(OWNERS, 1, 128)

    def place(p):
        return p % 16 * 8 + p // 16

    @pl.loop(1, OWNERS)
    def _(k):
        to = (pulse + k) % OWNERS
        pltpu.make_async_remote_copy(
            fsnd.at[to], frcv.at[place(pulse)], fsend, frecv, device_id=(to, y), device_id_type=MESH
        ).start()

    frcv[place(pulse)] = fsnd[pulse]
    final = pltpu.make_async_remote_copy(
        fsnd.at[pl.ds(0, OWNERS - 1)], frcv.at[pl.ds(0, OWNERS - 1)], fsend, frecv,
        device_id=plane_peer(1)[0], device_id_type=MESH,
    )
    final.wait_recv()
    arrived = frcv[...].reshape(OWNERS, 128)
    parts = split3(arrived)
    row = lax.broadcasted_iota(jnp.int32, (OWNERS, 128), 0)
    lane = lax.broadcasted_iota(jnp.int32, (OWNERS, 128), 1)
    own_lane = row // 8 == lane // 8
    for v in range(10):
        wide = sum(
            jnp.dot(part, pick[:, v * 128 : (v + 1) * 128], preferred_element_type=F32) for part in parts
        )
        out[v] = jnp.sum(jnp.where(own_lane, wide, 0.0).reshape(16, 8, 128), axis=0)

    for h in range(2):
        plane_all(h, PLANE - 1).wait_send()

        @pl.loop(1, NZ)
        def _(k):
            pltpu.make_async_remote_copy(
                zsnd.at[h, 0], zrcv.at[h, 0], zsend.at[h], zrecv.at[h, 0],
                device_id=z_peer(1)[0], device_id_type=MESH,
            ).wait_send()

        gather(h, "wait")
    final.wait_send()


def on_device(echoes, interp_weights, band_starts, row_lo, row_len, tile_owner):
    vmem = pl.BlockSpec(memory_space=pltpu.VMEM)
    hbm = pl.BlockSpec(memory_space=pl.ANY)
    sel, before, spread, pick = selectors()
    dma = pltpu.SemaphoreType.DMA
    annulus = resample(echoes.reshape(2, 16, 8192), interp_weights, band_starts, row_lo, row_len)
    moments = pl.pallas_call(
        body,
        out_shape=jax.ShapeDtypeStruct((10, 8, 128), F32),
        in_specs=[hbm, vmem, hbm, vmem, vmem, vmem, vmem],
        out_specs=vmem,
        scratch_shapes=[
            pltpu.VMEM((NZ, ROWS, 256), BF16),
            pltpu.VMEM((2, PLANE, 2, 16, 128), BF16),
            pltpu.VMEM((2, NZ, 3, 16, 128), BF16),
            pltpu.VMEM((2, NZ, 3, 16, 128), BF16),
            pltpu.VMEM((ROWS, 128), F32),
            pltpu.VMEM((128, 640), F32),
            pltpu.VMEM((2, 2, 16, 128), F32),
            pltpu.VMEM((8, 16, 128), F32),
            pltpu.VMEM((OWNERS, TILES), BF16),
            pltpu.VMEM((TILES, 128), F32),
            pltpu.VMEM((OWNERS, 1, 128), F32),
            pltpu.VMEM((OWNERS, 1, 128), F32),
            dma, dma((2,)), dma((2,)), dma((2,)), dma((2, NZ)), dma, dma, dma, dma,
        ],
        compiler_params=pltpu.CompilerParams(
            collective_id=0, has_side_effects=True, vmem_limit_bytes=48 * 1024 * 1024
        ),
    )(
        annulus,
        tile_owner.reshape(1, TILES),
        jnp.asarray(tables()),
        *[jnp.asarray(a) for a in (sel, before, spread, pick)],
    )
    return moments.reshape(10, 1, 1, 1024)


def solution(mesh):
    return jax.shard_map(
        on_device,
        mesh=mesh,
        in_specs=(
            P(None, "pol", "pulse", None),
            P(),
            P(),
            P("pulse"),
            P("pulse"),
            P("pol", "pulse", None, None),
        ),
        out_specs=P(None, "pol", "pulse", None),
        check_vma=False,
    )
```

```python
import math

import jax
import jax.numpy as jnp
import ml_dtypes
import numpy as np
from jax import lax
from jax.experimental import pallas as pl
from jax.experimental.pallas import tpu as pltpu
from jax.sharding import PartitionSpec as P

MESH = pl.DeviceIdType.MESH
ROOT_HALF = 1.0 / math.sqrt(2.0)
EPSILON = 1e-06
F32 = jnp.float32
BF16 = jnp.bfloat16

NX, NY, NZ, NC = 4, 4, 16, 2
PLANE = NX * NY * NC
GROUP = NX * NC
PULSES = 2048
ROWS = 1024
OWNERS = 128
TILES = 512
STEP = 16
BATCH = 4
VMEM_LIMIT = 60 * 1024 * 1024


def tables():
    row = np.arange(ROWS)
    azimuth = (row // 64 * 8 + row % 8) * 8 + row % 64 // 8
    z = np.arange(NZ)[:, None]
    k = np.arange(128)[None, :]
    pulse = (k // 32) * 512 + z * 32 + (k // 16 % 2) * 16 + k % 16
    m = azimuth[None, :, None] * pulse[:, None, :] % PULSES
    angles = m.astype(np.float32) * np.float32(2.0 * math.pi / PULSES)
    factor = np.float32(1.0 / math.sqrt(PULSES))
    both = np.concatenate([np.cos(angles) * factor, np.sin(angles) * factor], axis=2)
    return both.astype(ml_dtypes.bfloat16)


def selectors():
    sel = np.zeros((2, 2, 8, 5, 2, 2, 4, 8), np.float32)
    for turn in range(2):
        for v in range(3):
            sel[turn, v % 2, v // 2, 0, :, turn, v] = 1
            sel[turn, 1, 4, 0, :, turn, v] = 1
        for v, same, crossed, first in ((3, 1, 3, 0), (5, 2, 4, 0), (7, 1, 3, 1)):
            sel[turn, 1, v // 2, same, :, turn, first] = 1
            sel[turn, 0, (v + 1) // 2, crossed, 1, turn, first] = 1
            sel[turn, 0, (v + 1) // 2, crossed, 0, turn, first] = -1
    sel = sel.reshape(32, 640) / 64.0
    before = np.triu(np.ones((TILES, TILES), np.float32), 1)
    lanes = np.arange(128)
    rows = np.arange(16)[:, None]
    spread = (rows % 8 * 2 + rows // 8 == lanes[None, :] // 8) & (rows % 8 < 5)
    pick = np.concatenate([lanes[:, None] == v * 8 + lanes[None, :] % 8 for v in range(10)], axis=1)
    return [a.astype(ml_dtypes.bfloat16) for a in (sel, before, spread, pick)]


def split3(value):
    high = value.astype(BF16)
    rest = value - high.astype(F32)
    mid = rest.astype(BF16)
    low = (rest - mid.astype(F32)).astype(BF16)
    return high, mid, low


def swap_pieces(tiles, widths):
    lane = lax.broadcasted_iota(jnp.int32, (16, 128), 1) // 8
    tiles = list(tiles)
    for w in widths:
        upper = (lane & w) != 0
        for i in range(len(tiles)):
            if i & w:
                continue
            a, b = tiles[i], tiles[i | w]
            if a is None and b is None:
                continue
            zero = jnp.zeros_like(b if a is None else a)
            a_down = zero if a is None else pltpu.roll(a, 128 - 8 * w, 1)
            b_up = zero if b is None else pltpu.roll(b, 8 * w, 1)
            tiles[i] = jnp.where(upper, b_up, zero if a is None else a)
            tiles[i | w] = jnp.where(upper, zero if b is None else b, a_down)
    return tiles


def resample_body(starts, lo, length, echo, weights, out, starts_s, lo_s, length_s, echo_v, weights_v, out_v, sem, wsem, osem):
    smalls = [
        pltpu.make_async_copy(source, target, sem.at[n])
        for n, (source, target) in enumerate(((starts, starts_s), (lo, lo_s), (length, length_s), (echo, echo_v)))
    ]
    weight_copies = [
        pltpu.make_async_copy(weights.at[pl.ds(n * STEP, STEP)], weights_v.at[pl.ds(n * STEP, STEP)], wsem.at[n])
        for n in range(64 // STEP)
    ]
    for copy in smalls + weight_copies:
        copy.start()
    for copy in smalls:
        copy.wait()
    row = lax.broadcasted_iota(jnp.int32, (16, 128), 0)
    lane = lax.broadcasted_iota(jnp.int32, (16, 128), 1)
    lane2 = lax.broadcasted_iota(jnp.int32, (32, 128), 1)
    first = jnp.zeros((16, 128), jnp.int32)
    last = jnp.zeros((16, 128), jnp.int32)
    for r in range(16):
        first = jnp.where(row == r, lo_s[r], first)
        last = jnp.where(row == r, lo_s[r] + length_s[r], last)
    out_copies = []
    for step in range(64 // STEP):
        weight_copies[step].wait()

        @pl.loop(0, STEP, unroll=8)
        def _(n):
            band = step * STEP + n
            start = starts_s[band]
            base = jnp.minimum(start // 128, 62) * 128
            shift = start - base
            window = echo_v[:, :, pl.ds(pl.multiple_of(base, 128), 256)].astype(F32).reshape(32, 256)
            turn = (128 - shift) % 128
            left = pltpu.roll(window[:, :128], turn, 1)
            right = pltpu.roll(window[:, 128:], turn, 1)
            samples = jnp.where(lane2 < 128 - shift, left, right).astype(BF16)
            values = jnp.dot(samples, weights_v[band], preferred_element_type=F32).reshape(2, 16, 128)
            bins = band * 128 + lane
            inside = (bins >= first) & (bins < last)
            out_v[band] = jnp.where(inside[None], values, 0.0).astype(BF16)

        copy = pltpu.make_async_copy(out_v.at[pl.ds(step * STEP, STEP)], out.at[pl.ds(step * STEP, STEP)], osem.at[step])
        copy.start()
        out_copies.append(copy)
    for copy in out_copies:
        copy.wait()


def resample(echo, weights, starts, lo, length):
    hbm = pl.BlockSpec(memory_space=pl.ANY)
    dma = pltpu.SemaphoreType.DMA
    return pl.pallas_call(
        resample_body,
        out_shape=jax.ShapeDtypeStruct((64, 2, 16, 128), BF16),
        in_specs=[hbm] * 5,
        out_specs=hbm,
        scratch_shapes=[
            pltpu.SMEM((64,), jnp.int32),
            pltpu.SMEM((16,), jnp.int32),
            pltpu.SMEM((16,), jnp.int32),
            pltpu.VMEM((2, 16, 8192), BF16),
            pltpu.VMEM((64, 128, 128), BF16),
            pltpu.VMEM((64, 2, 16, 128), BF16),
            dma((4,)),
            dma((64 // STEP,)),
            dma((64 // STEP,)),
        ],
        compiler_params=pltpu.CompilerParams(vmem_limit_bytes=VMEM_LIMIT),
    )(starts, lo, length, echo, weights)


def body(
    snd, owner_h, table, sel_h, before_h, spread_h, pick_h,
    out,
    owner, tv, sel, before, spread, pick, prcv, zsnd, zrcv, acc, sums, vout, grcv, onehot, slotmask, fsnd, frcv,
    load_sem, psend, precv, zsend, zrecv, gsend, grecv, fsend, frecv,
):
    pulse = lax.axis_index("pulse")
    y = lax.axis_index("pol")
    x, z, core = pulse // 32, pulse // 2 % 16, pulse % 2
    rank = x * 8 + y * 2 + core

    def plane_peer(k):
        k = k * 5 % PLANE
        px, py, pc = (x + k // 8) % 4, (y + k // 2 % 4) % 4, (core + k) % 2
        return ((px * 16 + z) * 2 + pc, py), px * 8 + py * 2 + pc

    def z_offset(k):
        step = (17 - k) // 2
        return jnp.where(k == 0, 0, jnp.where(k % 2 == 1, step, 16 - step))

    def z_peer(k):
        pz = (z + z_offset(k)) % 16
        return ((x * 16 + pz) * 2 + core, y), pz

    loads = [
        pltpu.make_async_copy(source, target, load_sem.at[n])
        for n, (source, target) in enumerate(
            ((owner_h, owner), (before_h, before), (sel_h, sel), (spread_h, spread), (pick_h, pick), (table, tv))
        )
    ]
    for load in loads:
        load.start()

    barrier = pltpu.get_barrier_semaphore()

    @pl.loop(1, PLANE)
    def _(k):
        pl.semaphore_signal(barrier, inc=1, device_id=plane_peer(k)[0], device_id_type=MESH)

    @pl.loop(1, NZ)
    def _(k):
        pl.semaphore_signal(barrier, inc=1, device_id=z_peer(k)[0], device_id_type=MESH)

    row16 = lax.broadcasted_iota(jnp.int32, (16, 128), 0)
    lane16 = lax.broadcasted_iota(jnp.int32, (16, 128), 1)
    row8 = lax.broadcasted_iota(jnp.int32, (8, 128), 0)
    lane8 = lax.broadcasted_iota(jnp.int32, (8, 128), 1)

    def plane_send(h):
        @pl.loop(1, PLANE)
        def _(k):
            device, to = plane_peer(k)
            pltpu.make_async_remote_copy(
                snd.at[2 * to + h], prcv.at[h, rank], psend.at[h], precv.at[h], device_id=device, device_id_type=MESH
            ).start()

        pltpu.make_async_copy(snd.at[2 * rank + h], prcv.at[h, rank], precv.at[h]).start()

    def plane_all(h, count):
        return pltpu.make_async_remote_copy(
            prcv.at[h, pl.ds(0, count)], prcv.at[h, pl.ds(0, count)], psend.at[h], precv.at[h],
            device_id=plane_peer(1)[0], device_id_type=MESH,
        )

    pl.semaphore_wait(barrier, PLANE - 1 + NZ - 1)
    plane_send(0)
    plane_send(1)

    def pack(h):
        plane_all(h, PLANE).wait_recv()
        for t in range(3):
            tiles = []
            for part in range(2):
                for g in range(GROUP):
                    def channel(q):
                        return prcv[h, g // 2 * 8 + q * 2 + g % 2, part].astype(F32)

                    if t == 0:
                        value = channel(0) + channel(3)
                    elif t == 1:
                        value = channel(0) - channel(3)
                    else:
                        value = channel(1) + channel(2)
                    tiles.append((value * ROOT_HALF).astype(BF16))
            for to, tile in enumerate(swap_pieces(tiles, (1, 2, 4, 8))):
                zsnd[h, to, t] = tile

        @pl.loop(1, NZ)
        def _(k):
            device, to = z_peer(k)
            pltpu.make_async_remote_copy(
                zsnd.at[h, to], zrcv.at[h, z], zsend.at[h], zrecv.at[h, z], device_id=device, device_id_type=MESH
            ).start()

        pltpu.make_async_copy(zsnd.at[h, z], zrcv.at[h, z], zrecv.at[h, z]).start()

    pack(0)
    pack(1)

    for load in loads:
        load.wait()
    names = owner[...] == lax.broadcasted_iota(jnp.int32, (OWNERS, TILES), 0)
    mine = jnp.where(names, 1.0, 0.0).astype(BF16)
    onehot[...] = mine
    earlier = jnp.dot(mine, before[...], preferred_element_type=F32)
    earlier = jnp.where(names, earlier, 0.0).astype(BF16)
    slot = lax.dot_general(
        earlier, jnp.ones((OWNERS, 128), BF16), (((0,), (0,)), ((), ())), preferred_element_type=F32
    )
    lane_slot = (lax.broadcasted_iota(jnp.int32, (TILES, 128), 1) % 8).astype(F32)
    slotmask[...] = jnp.where(slot == lane_slot, 1.0, 0.0)

    sign_row = (1 - 2 * (row16 % 2)).astype(BF16)
    sign_part = jnp.where(lane16 < 64, 1.0, -1.0).astype(BF16)

    def samples_of(h, source):
        tiles = [zrcv[h, source, t] for t in range(3)] + [None] * 5
        plain, turned = [], []
        for tile in swap_pieces(tiles, (1, 2, 4)):
            tile = tile + pltpu.roll(tile, 32, 1) * sign_row
            plain.append(tile)
            turned.append(pltpu.roll(tile, 64, 1) * sign_part)
        return plain + turned

    def form(h):
        acc[...] = jnp.zeros_like(acc)

        @pl.loop(0, NZ // BATCH)
        def _(group):
            samples, waves = [], []
            for n in range(BATCH):
                source = (z + 16 - z_offset(group * BATCH + n)) % 16
                pltpu.make_async_remote_copy(
                    zsnd.at[h, 0], zrcv.at[h, source], zsend.at[h], zrecv.at[h, source],
                    device_id=z_peer(1)[0], device_id_type=MESH,
                ).wait_recv()
            for n in range(BATCH):
                source = (z + 16 - z_offset(group * BATCH + n)) % 16
                samples += samples_of(h, source)
                waves.append(tv[source])
            acc[...] += jnp.dot(
                jnp.concatenate(waves, axis=1), jnp.concatenate(samples, axis=0), preferred_element_type=F32
            )

        @pl.loop(0, ROWS // 64, unroll=4)
        def _(k):
            a = acc[pl.ds(pl.multiple_of(k * 64, 64), 64), :]
            b1 = pltpu.roll(a, 120, 1)
            b2 = pltpu.roll(a, 112, 1)
            others = (a, b1, b2, pltpu.roll(b1, 64, 1), pltpu.roll(b2, 64, 1))
            for n, other in enumerate(others):
                sums[pl.ds(pl.multiple_of(k * 8, 8), 8), n * 128 : (n + 1) * 128] = jnp.sum(
                    (a * other).reshape(8, 8, 128), axis=0
                )

        entries = sum(
            lax.dot_general(sel[...], part, (((1,), (1,)), ((), ())), preferred_element_type=F32)
            for part in split3(sums[...])
        )
        for turn in range(2):
            even, odd = entries[turn * 16 : turn * 16 + 8], entries[turn * 16 + 8 : turn * 16 + 16]
            scale = 1.0 / (odd[4:5] + EPSILON)
            even = even * scale
            odd = jnp.where(row8 == 4, odd, odd * scale)
            vout[h, 2 - 2 * turn] = jnp.where(lane8 < 64, even, pltpu.roll(odd, 64, 1))
            vout[h, 3 - 2 * turn] = jnp.where(lane8 < 64, pltpu.roll(even, 64, 1), odd)

    def gather(h, action):
        for g in range(NY):
            device = (x * 32 + (y * 4 + core * 2 + h) * 2 + z // 8, jnp.int32(g))
            here = (device[0] == pulse) & (y == g)
            source, target = vout.at[h, g], grcv.at[z % 8]

            @pl.when(jnp.logical_not(here))
            def _():
                copy = pltpu.make_async_remote_copy(
                    source, target, gsend, grecv, device_id=device, device_id_type=MESH
                )
                if action == "start":
                    copy.start()
                else:
                    copy.wait_send()

            if action == "start":

                @pl.when(here)
                def _():
                    pltpu.make_async_copy(source, target, grecv).start()

    for h in range(2):
        form(h)
        gather(h, "start")

    pltpu.make_async_remote_copy(grcv, grcv, gsend, grecv, device_id=plane_peer(1)[0], device_id_type=MESH).wait_recv()
    evens, odds = [], []
    for n in range(4):
        one, two = grcv[2 * n], grcv[2 * n + 1]
        evens.append(jnp.where(lane8 < 64, one, pltpu.roll(two, 64, 1)))
        odds.append(jnp.where(lane8 < 64, pltpu.roll(one, 64, 1), two))
    values = jnp.concatenate([jnp.concatenate(evens, axis=1), jnp.concatenate(odds, axis=1)], axis=0)
    wide = sum(
        lax.dot_general(part, spread[...], (((0,), (0,)), ((), ())), preferred_element_type=F32)
        for part in split3(values)
    )
    dealt = sum(
        jnp.dot(onehot[...], part, preferred_element_type=F32) for part in split3(wide * slotmask[...])
    )
    fsnd[...] = dealt.reshape(OWNERS, 1, 128)

    def place(p):
        return p % 16 * 8 + p // 16

    @pl.loop(1, OWNERS)
    def _(k):
        to = (pulse + k) % OWNERS
        pltpu.make_async_remote_copy(
            fsnd.at[to], frcv.at[place(pulse)], fsend, frecv, device_id=(to, y), device_id_type=MESH
        ).start()

    frcv[place(pulse)] = fsnd[pulse]
    final = pltpu.make_async_remote_copy(
        fsnd.at[pl.ds(0, OWNERS - 1)], frcv.at[pl.ds(0, OWNERS - 1)], fsend, frecv,
        device_id=plane_peer(1)[0], device_id_type=MESH,
    )
    final.wait_recv()
    arrived = frcv[...].reshape(OWNERS, 128)
    parts = split3(arrived)
    row = lax.broadcasted_iota(jnp.int32, (OWNERS, 128), 0)
    lane = lax.broadcasted_iota(jnp.int32, (OWNERS, 128), 1)
    own_lane = row // 8 == lane // 8
    for v in range(10):
        wide = sum(
            jnp.dot(part, pick[:, v * 128 : (v + 1) * 128], preferred_element_type=F32) for part in parts
        )
        out[v] = jnp.sum(jnp.where(own_lane, wide, 0.0).reshape(16, 8, 128), axis=0)

    for h in range(2):
        plane_all(h, PLANE - 1).wait_send()

        @pl.loop(1, NZ)
        def _(k):
            pltpu.make_async_remote_copy(
                zsnd.at[h, 0], zrcv.at[h, 0], zsend.at[h], zrecv.at[h, 0],
                device_id=z_peer(1)[0], device_id_type=MESH,
            ).wait_send()

        gather(h, "wait")
    final.wait_send()


def on_device(echoes, interp_weights, band_starts, row_lo, row_len, tile_owner):
    vmem = pl.BlockSpec(memory_space=pltpu.VMEM)
    hbm = pl.BlockSpec(memory_space=pl.ANY)
    sel, before, spread, pick = selectors()
    dma = pltpu.SemaphoreType.DMA
    annulus = resample(echoes.reshape(2, 16, 8192), interp_weights, band_starts, row_lo, row_len)
    moments = pl.pallas_call(
        body,
        out_shape=jax.ShapeDtypeStruct((10, 8, 128), F32),
        in_specs=[hbm] * 7,
        out_specs=vmem,
        scratch_shapes=[
            pltpu.VMEM((1, TILES), jnp.int32),
            pltpu.VMEM((NZ, ROWS, 256), BF16),
            pltpu.VMEM((32, 640), BF16),
            pltpu.VMEM((TILES, TILES), BF16),
            pltpu.VMEM((16, 128), BF16),
            pltpu.VMEM((128, 1280), BF16),
            pltpu.VMEM((2, PLANE, 2, 16, 128), BF16),
            pltpu.VMEM((2, NZ, 3, 16, 128), BF16),
            pltpu.VMEM((2, NZ, 3, 16, 128), BF16),
            pltpu.VMEM((ROWS, 128), F32),
            pltpu.VMEM((128, 640), F32),
            pltpu.VMEM((2, NY, 8, 128), F32),
            pltpu.VMEM((8, 8, 128), F32),
            pltpu.VMEM((OWNERS, TILES), BF16),
            pltpu.VMEM((TILES, 128), F32),
            pltpu.VMEM((OWNERS, 1, 128), F32),
            pltpu.VMEM((OWNERS, 1, 128), F32),
            dma((6,)), dma((2,)), dma((2,)), dma((2,)), dma((2, NZ)), dma, dma, dma, dma,
        ],
        compiler_params=pltpu.CompilerParams(
            collective_id=0, has_side_effects=True, vmem_limit_bytes=VMEM_LIMIT
        ),
    )(
        annulus,
        tile_owner.reshape(1, TILES),
        jnp.asarray(tables()),
        *[jnp.asarray(a) for a in (sel, before, spread, pick)],
    )
    return moments.reshape(10, 1, 1, 1024)


def solution(mesh):
    return jax.shard_map(
        on_device,
        mesh=mesh,
        in_specs=(
            P(None, "pol", "pulse", None),
            P(),
            P(),
            P("pulse"),
            P("pulse"),
            P("pol", "pulse", None, None),
        ),
        out_specs=P(None, "pol", "pulse", None),
        check_vma=False,
    )
```

```python
import math

import jax
import jax.numpy as jnp
import ml_dtypes
import numpy as np
from jax import lax
from jax.experimental import pallas as pl
from jax.experimental.pallas import tpu as pltpu
from jax.sharding import PartitionSpec as P

MESH = pl.DeviceIdType.MESH
ROOT_HALF = 1.0 / math.sqrt(2.0)
EPSILON = 1e-06
F32 = jnp.float32
BF16 = jnp.bfloat16

NX, NY, NZ, NC = 4, 4, 16, 2
PLANE = NX * NY * NC
GROUP = NX * NC
PULSES = 2048
ROWS = 1024
OWNERS = 128
TILES = 512
STEP = 16
BATCH = 4
VMEM_LIMIT = 60 * 1024 * 1024


def tables():
    row = np.arange(ROWS)
    azimuth = (row // 64 * 8 + row % 8) * 8 + row % 64 // 8
    z = np.arange(NZ)[:, None]
    k = np.arange(128)[None, :]
    pulse = (k // 32) * 512 + z * 32 + (k // 16 % 2) * 16 + k % 16
    m = azimuth[None, :, None] * pulse[:, None, :] % PULSES
    angles = m.astype(np.float32) * np.float32(2.0 * math.pi / PULSES)
    factor = np.float32(1.0 / math.sqrt(PULSES))
    both = np.concatenate([np.cos(angles) * factor, np.sin(angles) * factor], axis=2)
    return both.astype(ml_dtypes.bfloat16)


def selectors():
    sel = np.zeros((2, 2, 8, 5, 2, 2, 4, 8), np.float32)
    for turn in range(2):
        for v in range(3):
            sel[turn, v % 2, v // 2, 0, :, turn, v] = 1
            sel[turn, 1, 4, 0, :, turn, v] = 1
        for v, same, crossed, first in ((3, 1, 3, 0), (5, 2, 4, 0), (7, 1, 3, 1)):
            sel[turn, 1, v // 2, same, :, turn, first] = 1
            sel[turn, 0, (v + 1) // 2, crossed, 1, turn, first] = 1
            sel[turn, 0, (v + 1) // 2, crossed, 0, turn, first] = -1
    sel = sel.reshape(32, 640) / 64.0
    before = np.triu(np.ones((TILES, TILES), np.float32), 1)
    lanes = np.arange(128)
    rows = np.arange(16)[:, None]
    spread = (rows % 8 * 2 + rows // 8 == lanes[None, :] // 8) & (rows % 8 < 5)
    pick = np.concatenate([lanes[:, None] == v * 8 + lanes[None, :] % 8 for v in range(10)], axis=1)
    return [a.astype(ml_dtypes.bfloat16) for a in (sel, before, spread, pick)]


def rem(a, b):
    return lax.rem(a, jnp.int32(b))


def div(a, b):
    return lax.div(a, jnp.int32(b))


def split3(value):
    high = value.astype(BF16)
    rest = value - high.astype(F32)
    mid = rest.astype(BF16)
    low = (rest - mid.astype(F32)).astype(BF16)
    return high, mid, low


def swap_pieces(tiles, widths):
    lane = lax.broadcasted_iota(jnp.int32, (16, 128), 1) // 8
    tiles = list(tiles)
    for w in widths:
        upper = (lane & w) != 0
        for i in range(len(tiles)):
            if i & w:
                continue
            a, b = tiles[i], tiles[i | w]
            if a is None and b is None:
                continue
            zero = jnp.zeros_like(b if a is None else a)
            a_down = zero if a is None else pltpu.roll(a, 128 - 8 * w, 1)
            b_up = zero if b is None else pltpu.roll(b, 8 * w, 1)
            tiles[i] = jnp.where(upper, b_up, zero if a is None else a)
            tiles[i | w] = jnp.where(upper, zero if b is None else b, a_down)
    return tiles


def resample_body(starts, lo, length, echo, weights, out, starts_s, lo_s, length_s, echo_v, weights_v, out_v, sem, wsem, osem):
    smalls = [
        pltpu.make_async_copy(source, target, sem.at[n])
        for n, (source, target) in enumerate(((starts, starts_s), (lo, lo_s), (length, length_s), (echo, echo_v)))
    ]
    weight_copies = [
        pltpu.make_async_copy(weights.at[pl.ds(n * STEP, STEP)], weights_v.at[pl.ds(n * STEP, STEP)], wsem.at[n])
        for n in range(64 // STEP)
    ]
    for copy in smalls + weight_copies:
        copy.start()
    for copy in smalls:
        copy.wait()
    row = lax.broadcasted_iota(jnp.int32, (16, 128), 0)
    lane = lax.broadcasted_iota(jnp.int32, (16, 128), 1)
    lane2 = lax.broadcasted_iota(jnp.int32, (32, 128), 1)
    first = jnp.zeros((16, 128), jnp.int32)
    last = jnp.zeros((16, 128), jnp.int32)
    for r in range(16):
        first = jnp.where(row == r, lo_s[r], first)
        last = jnp.where(row == r, lo_s[r] + length_s[r], last)
    out_copies = []
    for step in range(64 // STEP):
        weight_copies[step].wait()

        @pl.loop(0, STEP, unroll=16)
        def _(n):
            band = step * STEP + n
            start = starts_s[band]
            base = jnp.minimum(start // 128, 62) * 128
            shift = start - base
            window = echo_v[:, :, pl.ds(pl.multiple_of(base, 128), 256)].astype(F32).reshape(32, 256)
            turn = (128 - shift) % 128
            left = pltpu.roll(window[:, :128], turn, 1)
            right = pltpu.roll(window[:, 128:], turn, 1)
            samples = jnp.where(lane2 < 128 - shift, left, right).astype(BF16)
            values = jnp.dot(samples, weights_v[band], preferred_element_type=F32).reshape(2, 16, 128)
            bins = band * 128 + lane
            inside = (bins >= first) & (bins < last)
            out_v[band] = jnp.where(inside[None], values, 0.0).astype(BF16)

        copy = pltpu.make_async_copy(out_v.at[pl.ds(step * STEP, STEP)], out.at[pl.ds(step * STEP, STEP)], osem.at[step])
        copy.start()
        out_copies.append(copy)
    for copy in out_copies:
        copy.wait()


def resample(echo, weights, starts, lo, length):
    hbm = pl.BlockSpec(memory_space=pl.ANY)
    dma = pltpu.SemaphoreType.DMA
    return pl.pallas_call(
        resample_body,
        out_shape=jax.ShapeDtypeStruct((64, 2, 16, 128), BF16),
        in_specs=[hbm] * 5,
        out_specs=hbm,
        scratch_shapes=[
            pltpu.SMEM((64,), jnp.int32),
            pltpu.SMEM((16,), jnp.int32),
            pltpu.SMEM((16,), jnp.int32),
            pltpu.VMEM((2, 16, 8192), BF16),
            pltpu.VMEM((64, 128, 128), BF16),
            pltpu.VMEM((64, 2, 16, 128), BF16),
            dma((4,)),
            dma((64 // STEP,)),
            dma((64 // STEP,)),
        ],
        compiler_params=pltpu.CompilerParams(vmem_limit_bytes=VMEM_LIMIT),
    )(starts, lo, length, echo, weights)


def body(
    snd, owner_h, table, sel_h, before_h, spread_h, pick_h,
    out,
    owner, tv, sel, before, spread, pick, prcv, zsnd, zrcv, acc, sums, vout, grcv, onehot, slotmask, fsnd, frcv,
    load_sem, psend, precv, zsend, zrecv, gsend, grecv, fsend, frecv,
):
    pulse = lax.axis_index("pulse")
    y = lax.axis_index("pol")
    x, z, core = pulse // 32, pulse // 2 % 16, pulse % 2
    rank = x * 8 + y * 2 + core

    def plane_peer(k):
        k = rem(jnp.int32(k) * 5, PLANE)
        px, py, pc = rem(x + div(k, 8), 4), rem(y + div(k, 2), 4), rem(core + k, 2)
        return ((px * 16 + z) * 2 + pc, py), px * 8 + py * 2 + pc

    def z_offset(k):
        k = jnp.int32(k)
        step = div(17 - k, 2)
        return jnp.where(k == 0, 0, jnp.where(rem(k, 2) == 1, step, 16 - step))

    def z_peer(k):
        pz = rem(z + z_offset(k), 16)
        return ((x * 16 + pz) * 2 + core, y), pz

    loads = [
        pltpu.make_async_copy(source, target, load_sem.at[n])
        for n, (source, target) in enumerate(
            ((owner_h, owner), (before_h, before), (sel_h, sel), (spread_h, spread), (pick_h, pick), (table, tv))
        )
    ]
    for load in loads:
        load.start()

    barrier = pltpu.get_barrier_semaphore()

    @pl.loop(1, PLANE)
    def _(k):
        pl.semaphore_signal(barrier, inc=1, device_id=plane_peer(k)[0], device_id_type=MESH)

    @pl.loop(1, NZ)
    def _(k):
        pl.semaphore_signal(barrier, inc=1, device_id=z_peer(k)[0], device_id_type=MESH)

    row16 = lax.broadcasted_iota(jnp.int32, (16, 128), 0)
    lane16 = lax.broadcasted_iota(jnp.int32, (16, 128), 1)
    row8 = lax.broadcasted_iota(jnp.int32, (8, 128), 0)
    lane8 = lax.broadcasted_iota(jnp.int32, (8, 128), 1)

    def plane_send(h):
        @pl.loop(1, PLANE)
        def _(k):
            device, to = plane_peer(k)
            pltpu.make_async_remote_copy(
                snd.at[2 * to + h], prcv.at[h, rank], psend.at[h], precv.at[h], device_id=device, device_id_type=MESH
            ).start()

        pltpu.make_async_copy(snd.at[2 * rank + h], prcv.at[h, rank], precv.at[h]).start()

    def plane_all(h, count):
        return pltpu.make_async_remote_copy(
            prcv.at[h, pl.ds(0, count)], prcv.at[h, pl.ds(0, count)], psend.at[h], precv.at[h],
            device_id=plane_peer(1)[0], device_id_type=MESH,
        )

    pl.semaphore_wait(barrier, PLANE - 1 + NZ - 1)
    plane_send(0)
    plane_send(1)

    def pack(h):
        plane_all(h, PLANE).wait_recv()
        for t in range(3):
            tiles = []
            for part in range(2):
                for g in range(GROUP):
                    def channel(q):
                        return prcv[h, g // 2 * 8 + q * 2 + g % 2, part].astype(F32)

                    if t == 0:
                        value = channel(0) + channel(3)
                    elif t == 1:
                        value = channel(0) - channel(3)
                    else:
                        value = channel(1) + channel(2)
                    tiles.append((value * ROOT_HALF).astype(BF16))
            for to, tile in enumerate(swap_pieces(tiles, (1, 2, 4, 8))):
                zsnd[h, to, t] = tile

        @pl.loop(1, NZ)
        def _(k):
            device, to = z_peer(k)
            pltpu.make_async_remote_copy(
                zsnd.at[h, to], zrcv.at[h, z], zsend.at[h], zrecv.at[h, z], device_id=device, device_id_type=MESH
            ).start()

        pltpu.make_async_copy(zsnd.at[h, z], zrcv.at[h, z], zrecv.at[h, z]).start()

    pack(0)
    pack(1)

    for load in loads:
        load.wait()
    names = owner[...] == lax.broadcasted_iota(jnp.int32, (OWNERS, TILES), 0)
    mine = jnp.where(names, 1.0, 0.0).astype(BF16)
    onehot[...] = mine
    earlier = jnp.dot(mine, before[...], preferred_element_type=F32)
    earlier = jnp.where(names, earlier, 0.0).astype(BF16)
    slot = lax.dot_general(
        earlier, jnp.ones((OWNERS, 128), BF16), (((0,), (0,)), ((), ())), preferred_element_type=F32
    )
    lane_slot = (lax.broadcasted_iota(jnp.int32, (TILES, 128), 1) % 8).astype(F32)
    slotmask[...] = jnp.where(slot == lane_slot, 1.0, 0.0)

    sign_row = (1 - 2 * (row16 % 2)).astype(BF16)
    sign_part = jnp.where(lane16 < 64, 1.0, -1.0).astype(BF16)

    def samples_of(h, source):
        tiles = [zrcv[h, source, t] for t in range(3)] + [None] * 5
        plain, turned = [], []
        for tile in swap_pieces(tiles, (1, 2, 4)):
            tile = tile + pltpu.roll(tile, 32, 1) * sign_row
            plain.append(tile)
            turned.append(pltpu.roll(tile, 64, 1) * sign_part)
        return plain + turned

    def form(h):
        acc[...] = jnp.zeros_like(acc)

        @pl.loop(0, NZ // BATCH)
        def _(group):
            samples, waves = [], []
            for n in range(BATCH):
                source = rem(z + 16 - z_offset(group * BATCH + n), 16)
                pltpu.make_async_remote_copy(
                    zsnd.at[h, 0], zrcv.at[h, source], zsend.at[h], zrecv.at[h, source],
                    device_id=z_peer(1)[0], device_id_type=MESH,
                ).wait_recv()
            for n in range(BATCH):
                source = rem(z + 16 - z_offset(group * BATCH + n), 16)
                samples += samples_of(h, source)
                waves.append(tv[source])
            acc[...] += jnp.dot(
                jnp.concatenate(waves, axis=1), jnp.concatenate(samples, axis=0), preferred_element_type=F32
            )

        @pl.loop(0, ROWS // 64, unroll=4)
        def _(k):
            a = acc[pl.ds(pl.multiple_of(k * 64, 64), 64), :]
            b1 = pltpu.roll(a, 120, 1)
            b2 = pltpu.roll(a, 112, 1)
            others = (a, b1, b2, pltpu.roll(b1, 64, 1), pltpu.roll(b2, 64, 1))
            for n, other in enumerate(others):
                sums[pl.ds(pl.multiple_of(k * 8, 8), 8), n * 128 : (n + 1) * 128] = jnp.sum(
                    (a * other).reshape(8, 8, 128), axis=0
                )

        entries = sum(
            lax.dot_general(sel[...], part, (((1,), (1,)), ((), ())), preferred_element_type=F32)
            for part in split3(sums[...])
        )
        for turn in range(2):
            even, odd = entries[turn * 16 : turn * 16 + 8], entries[turn * 16 + 8 : turn * 16 + 16]
            scale = 1.0 / (odd[4:5] + EPSILON)
            even = even * scale
            odd = jnp.where(row8 == 4, odd, odd * scale)
            vout[h, 2 - 2 * turn] = jnp.where(lane8 < 64, even, pltpu.roll(odd, 64, 1))
            vout[h, 3 - 2 * turn] = jnp.where(lane8 < 64, pltpu.roll(even, 64, 1), odd)

    def gather(h, action):
        for g in range(NY):
            device = (x * 32 + (y * 4 + core * 2 + h) * 2 + z // 8, jnp.int32(g))
            here = (device[0] == pulse) & (y == g)
            source, target = vout.at[h, g], grcv.at[z % 8]

            @pl.when(jnp.logical_not(here))
            def _():
                copy = pltpu.make_async_remote_copy(
                    source, target, gsend, grecv, device_id=device, device_id_type=MESH
                )
                if action == "start":
                    copy.start()
                else:
                    copy.wait_send()

            if action == "start":

                @pl.when(here)
                def _():
                    pltpu.make_async_copy(source, target, grecv).start()

    for h in range(2):
        form(h)
        gather(h, "start")

    pltpu.make_async_remote_copy(grcv, grcv, gsend, grecv, device_id=plane_peer(1)[0], device_id_type=MESH).wait_recv()
    evens, odds = [], []
    for n in range(4):
        one, two = grcv[2 * n], grcv[2 * n + 1]
        evens.append(jnp.where(lane8 < 64, one, pltpu.roll(two, 64, 1)))
        odds.append(jnp.where(lane8 < 64, pltpu.roll(one, 64, 1), two))
    values = jnp.concatenate([jnp.concatenate(evens, axis=1), jnp.concatenate(odds, axis=1)], axis=0)
    wide = sum(
        lax.dot_general(part, spread[...], (((0,), (0,)), ((), ())), preferred_element_type=F32)
        for part in split3(values)
    )
    dealt = sum(
        jnp.dot(onehot[...], part, preferred_element_type=F32) for part in split3(wide * slotmask[...])
    )
    fsnd[...] = dealt.reshape(OWNERS, 1, 128)

    def place(p):
        return p % 16 * 8 + p // 16

    here = place(pulse)

    @pl.loop(1, OWNERS)
    def _(k):
        to = rem(pulse + k, OWNERS)
        pltpu.make_async_remote_copy(
            fsnd.at[to], frcv.at[here], fsend, frecv, device_id=(to, y), device_id_type=MESH
        ).start()

    frcv[here] = fsnd[pulse]
    final = pltpu.make_async_remote_copy(
        fsnd.at[pl.ds(0, OWNERS - 1)], frcv.at[pl.ds(0, OWNERS - 1)], fsend, frecv,
        device_id=plane_peer(1)[0], device_id_type=MESH,
    )
    final.wait_recv()
    arrived = frcv[...].reshape(OWNERS, 128)
    parts = split3(arrived)
    row = lax.broadcasted_iota(jnp.int32, (OWNERS, 128), 0)
    lane = lax.broadcasted_iota(jnp.int32, (OWNERS, 128), 1)
    own_lane = row // 8 == lane // 8
    for v in range(10):
        wide = sum(
            jnp.dot(part, pick[:, v * 128 : (v + 1) * 128], preferred_element_type=F32) for part in parts
        )
        out[v] = jnp.sum(jnp.where(own_lane, wide, 0.0).reshape(16, 8, 128), axis=0)

    for h in range(2):
        plane_all(h, PLANE - 1).wait_send()

        @pl.loop(1, NZ)
        def _(k):
            pltpu.make_async_remote_copy(
                zsnd.at[h, 0], zrcv.at[h, 0], zsend.at[h], zrecv.at[h, 0],
                device_id=z_peer(1)[0], device_id_type=MESH,
            ).wait_send()

        gather(h, "wait")
    final.wait_send()


def on_device(echoes, interp_weights, band_starts, row_lo, row_len, tile_owner):
    vmem = pl.BlockSpec(memory_space=pltpu.VMEM)
    hbm = pl.BlockSpec(memory_space=pl.ANY)
    sel, before, spread, pick = selectors()
    dma = pltpu.SemaphoreType.DMA
    annulus = resample(echoes.reshape(2, 16, 8192), interp_weights, band_starts, row_lo, row_len)
    moments = pl.pallas_call(
        body,
        out_shape=jax.ShapeDtypeStruct((10, 8, 128), F32),
        in_specs=[hbm] * 7,
        out_specs=vmem,
        scratch_shapes=[
            pltpu.VMEM((1, TILES), jnp.int32),
            pltpu.VMEM((NZ, ROWS, 256), BF16),
            pltpu.VMEM((32, 640), BF16),
            pltpu.VMEM((TILES, TILES), BF16),
            pltpu.VMEM((16, 128), BF16),
            pltpu.VMEM((128, 1280), BF16),
            pltpu.VMEM((2, PLANE, 2, 16, 128), BF16),
            pltpu.VMEM((2, NZ, 3, 16, 128), BF16),
            pltpu.VMEM((2, NZ, 3, 16, 128), BF16),
            pltpu.VMEM((ROWS, 128), F32),
            pltpu.VMEM((128, 640), F32),
            pltpu.VMEM((2, NY, 8, 128), F32),
            pltpu.VMEM((8, 8, 128), F32),
            pltpu.VMEM((OWNERS, TILES), BF16),
            pltpu.VMEM((TILES, 128), F32),
            pltpu.VMEM((OWNERS, 1, 128), F32),
            pltpu.VMEM((OWNERS, 1, 128), F32),
            dma((6,)), dma((2,)), dma((2,)), dma((2,)), dma((2, NZ)), dma, dma, dma, dma,
        ],
        compiler_params=pltpu.CompilerParams(
            collective_id=0, has_side_effects=True, vmem_limit_bytes=VMEM_LIMIT
        ),
    )(
        annulus,
        tile_owner.reshape(1, TILES),
        jnp.asarray(tables()),
        *[jnp.asarray(a) for a in (sel, before, spread, pick)],
    )
    return moments.reshape(10, 1, 1, 1024)


def solution(mesh):
    return jax.shard_map(
        on_device,
        mesh=mesh,
        in_specs=(
            P(None, "pol", "pulse", None),
            P(),
            P(),
            P("pulse"),
            P("pulse"),
            P("pol", "pulse", None, None),
        ),
        out_specs=P(None, "pol", "pulse", None),
        check_vma=False,
    )
```

```python
import math

import jax
import jax.numpy as jnp
import ml_dtypes
import numpy as np
from jax import lax
from jax.experimental import pallas as pl
from jax.experimental.pallas import tpu as pltpu
from jax.sharding import PartitionSpec as P

MESH = pl.DeviceIdType.MESH
ROOT_HALF = 1.0 / math.sqrt(2.0)
EPSILON = 1e-06
F32 = jnp.float32
BF16 = jnp.bfloat16

NX, NY, NZ, NC = 4, 4, 16, 2
PLANE = NX * NY * NC
GROUP = NX * NC
PULSES = 2048
ROWS = 1024
OWNERS = 128
TILES = 512
STEP = 16
BATCH = 4
VMEM_LIMIT = 60 * 1024 * 1024


def tables():
    row = np.arange(ROWS)
    azimuth = (row // 64 * 8 + row % 8) * 8 + row % 64 // 8
    z = np.arange(NZ)[:, None]
    k = np.arange(128)[None, :]
    pulse = (k // 32) * 512 + z * 32 + (k // 16 % 2) * 16 + k % 16
    m = azimuth[None, :, None] * pulse[:, None, :] % PULSES
    angles = m.astype(np.float32) * np.float32(2.0 * math.pi / PULSES)
    factor = np.float32(1.0 / math.sqrt(PULSES))
    both = np.concatenate([np.cos(angles) * factor, np.sin(angles) * factor], axis=2)
    return both.astype(ml_dtypes.bfloat16)


def selectors():
    sel = np.zeros((2, 2, 8, 5, 2, 2, 4, 8), np.float32)
    for turn in range(2):
        for v in range(3):
            sel[turn, v % 2, v // 2, 0, :, turn, v] = 1
            sel[turn, 1, 4, 0, :, turn, v] = 1
        for v, same, crossed, first in ((3, 1, 3, 0), (5, 2, 4, 0), (7, 1, 3, 1)):
            sel[turn, 1, v // 2, same, :, turn, first] = 1
            sel[turn, 0, (v + 1) // 2, crossed, 1, turn, first] = 1
            sel[turn, 0, (v + 1) // 2, crossed, 0, turn, first] = -1
    sel = sel.reshape(32, 640) / 64.0
    before = np.triu(np.ones((TILES, TILES), np.float32), 1)
    lanes = np.arange(128)
    rows = np.arange(16)[:, None]
    spread = (rows % 8 * 2 + rows // 8 == lanes[None, :] // 8) & (rows % 8 < 5)
    pick = np.concatenate([lanes[:, None] == v * 8 + lanes[None, :] % 8 for v in range(10)], axis=1)
    return [a.astype(ml_dtypes.bfloat16) for a in (sel, before, spread, pick)]


def rem(a, b):
    return lax.rem(a, jnp.int32(b))


def div(a, b):
    return lax.div(a, jnp.int32(b))


def split3(value):
    high = value.astype(BF16)
    rest = value - high.astype(F32)
    mid = rest.astype(BF16)
    low = (rest - mid.astype(F32)).astype(BF16)
    return high, mid, low


def swap_pieces(tiles, widths):
    lane = lax.broadcasted_iota(jnp.int32, (16, 128), 1) // 8
    tiles = list(tiles)
    for w in widths:
        upper = (lane & w) != 0
        for i in range(len(tiles)):
            if i & w:
                continue
            a, b = tiles[i], tiles[i | w]
            if a is None and b is None:
                continue
            zero = jnp.zeros_like(b if a is None else a)
            a_down = zero if a is None else pltpu.roll(a, 128 - 8 * w, 1)
            b_up = zero if b is None else pltpu.roll(b, 8 * w, 1)
            tiles[i] = jnp.where(upper, b_up, zero if a is None else a)
            tiles[i | w] = jnp.where(upper, zero if b is None else b, a_down)
    return tiles


def resample_body(starts, lo, length, echo, weights, out, starts_s, lo_s, length_s, echo_v, weights_v, out_v, sem, wsem, osem):
    smalls = [
        pltpu.make_async_copy(source, target, sem.at[n])
        for n, (source, target) in enumerate(((starts, starts_s), (lo, lo_s), (length, length_s), (echo, echo_v)))
    ]
    weight_copies = [
        pltpu.make_async_copy(weights.at[pl.ds(n * STEP, STEP)], weights_v.at[pl.ds(n * STEP, STEP)], wsem.at[n])
        for n in range(64 // STEP)
    ]
    for copy in smalls + weight_copies:
        copy.start()
    for copy in smalls:
        copy.wait()
    row = lax.broadcasted_iota(jnp.int32, (16, 128), 0)
    lane = lax.broadcasted_iota(jnp.int32, (16, 128), 1)
    lane2 = lax.broadcasted_iota(jnp.int32, (32, 128), 1)
    first = jnp.zeros((16, 128), jnp.int32)
    last = jnp.zeros((16, 128), jnp.int32)
    for r in range(16):
        first = jnp.where(row == r, lo_s[r], first)
        last = jnp.where(row == r, lo_s[r] + length_s[r], last)
    out_copies = []
    for step in range(64 // STEP):
        weight_copies[step].wait()

        @pl.loop(0, STEP, unroll=16)
        def _(n):
            band = step * STEP + n
            start = starts_s[band]
            base = jnp.minimum(start // 128, 62) * 128
            shift = start - base
            window = echo_v[:, :, pl.ds(pl.multiple_of(base, 128), 256)].astype(F32).reshape(32, 256)
            turn = (128 - shift) % 128
            left = pltpu.roll(window[:, :128], turn, 1)
            right = pltpu.roll(window[:, 128:], turn, 1)
            samples = jnp.where(lane2 < 128 - shift, left, right).astype(BF16)
            values = jnp.dot(samples, weights_v[band], preferred_element_type=F32).reshape(2, 16, 128)
            bins = band * 128 + lane
            inside = (bins >= first) & (bins < last)
            out_v[band] = jnp.where(inside[None], values, 0.0).astype(BF16)

        copy = pltpu.make_async_copy(out_v.at[pl.ds(step * STEP, STEP)], out.at[pl.ds(step * STEP, STEP)], osem.at[step])
        copy.start()
        out_copies.append(copy)
    for copy in out_copies:
        copy.wait()


def resample(echo, weights, starts, lo, length):
    hbm = pl.BlockSpec(memory_space=pl.ANY)
    dma = pltpu.SemaphoreType.DMA
    return pl.pallas_call(
        resample_body,
        out_shape=jax.ShapeDtypeStruct((64, 2, 16, 128), BF16),
        in_specs=[hbm] * 5,
        out_specs=hbm,
        scratch_shapes=[
            pltpu.SMEM((64,), jnp.int32),
            pltpu.SMEM((16,), jnp.int32),
            pltpu.SMEM((16,), jnp.int32),
            pltpu.VMEM((2, 16, 8192), BF16),
            pltpu.VMEM((64, 128, 128), BF16),
            pltpu.VMEM((64, 2, 16, 128), BF16),
            dma((4,)),
            dma((64 // STEP,)),
            dma((64 // STEP,)),
        ],
        compiler_params=pltpu.CompilerParams(vmem_limit_bytes=VMEM_LIMIT),
    )(starts, lo, length, echo, weights)


def body(
    snd, owner_h, table, sel_h, before_h, spread_h, pick_h,
    out,
    owner, tv, sel, before, spread, pick, prcv, zsnd, zrcv, acc, sums, vout, grcv, onehot, slotmask, fsnd, frcv,
    load_sem, psend, precv, zsend, zrecv, gsend, grecv, fsend, frecv,
):
    pulse = lax.axis_index("pulse")
    y = lax.axis_index("pol")
    x, z, core = pulse // 32, pulse // 2 % 16, pulse % 2
    rank = x * 8 + y * 2 + core

    def plane_peer(k):
        k = rem(jnp.int32(k) * 5, PLANE)
        px, py, pc = rem(x + div(k, 8), 4), rem(y + div(k, 2), 4), rem(core + k, 2)
        return ((px * 16 + z) * 2 + pc, py), px * 8 + py * 2 + pc

    def z_offset(k):
        k = jnp.int32(k)
        step = div(17 - k, 2)
        return jnp.where(k == 0, 0, jnp.where(rem(k, 2) == 1, step, 16 - step))

    def z_peer(k):
        pz = rem(z + z_offset(k), 16)
        return ((x * 16 + pz) * 2 + core, y), pz

    loads = [
        pltpu.make_async_copy(source, target, load_sem.at[n])
        for n, (source, target) in enumerate(
            ((owner_h, owner), (before_h, before), (sel_h, sel), (spread_h, spread), (pick_h, pick), (table, tv))
        )
    ]
    for load in loads:
        load.start()

    barrier = pltpu.get_barrier_semaphore()

    @pl.loop(1, PLANE)
    def _(k):
        pl.semaphore_signal(barrier, inc=1, device_id=plane_peer(k)[0], device_id_type=MESH)

    @pl.loop(1, NZ)
    def _(k):
        pl.semaphore_signal(barrier, inc=1, device_id=z_peer(k)[0], device_id_type=MESH)

    row16 = lax.broadcasted_iota(jnp.int32, (16, 128), 0)
    lane16 = lax.broadcasted_iota(jnp.int32, (16, 128), 1)
    row8 = lax.broadcasted_iota(jnp.int32, (8, 128), 0)
    lane8 = lax.broadcasted_iota(jnp.int32, (8, 128), 1)

    def plane_send(h):
        @pl.loop(1, PLANE)
        def _(k):
            device, to = plane_peer(k)
            pltpu.make_async_remote_copy(
                snd.at[2 * to + h], prcv.at[h, rank], psend.at[h], precv.at[h], device_id=device, device_id_type=MESH
            ).start()

        pltpu.make_async_copy(snd.at[2 * rank + h], prcv.at[h, rank], precv.at[h]).start()

    def plane_all(h, count):
        return pltpu.make_async_remote_copy(
            prcv.at[h, pl.ds(0, count)], prcv.at[h, pl.ds(0, count)], psend.at[h], precv.at[h],
            device_id=plane_peer(1)[0], device_id_type=MESH,
        )

    pl.semaphore_wait(barrier, PLANE - 1 + NZ - 1)
    plane_send(0)
    plane_send(1)

    def pack(h):
        plane_all(h, PLANE).wait_recv()
        for t in range(3):
            tiles = []
            for part in range(2):
                for g in range(GROUP):
                    def channel(q):
                        return prcv[h, g // 2 * 8 + q * 2 + g % 2, part].astype(F32)

                    if t == 0:
                        value = channel(0) + channel(3)
                    elif t == 1:
                        value = channel(0) - channel(3)
                    else:
                        value = channel(1) + channel(2)
                    tiles.append((value * ROOT_HALF).astype(BF16))
            for to, tile in enumerate(swap_pieces(tiles, (1, 2, 4, 8))):
                zsnd[h, to, t] = tile

        @pl.loop(1, NZ)
        def _(k):
            device, to = z_peer(k)
            pltpu.make_async_remote_copy(
                zsnd.at[h, to], zrcv.at[h, z], zsend.at[h], zrecv.at[h, z], device_id=device, device_id_type=MESH
            ).start()

        pltpu.make_async_copy(zsnd.at[h, z], zrcv.at[h, z], zrecv.at[h, z]).start()

    pack(0)
    pack(1)

    for load in loads:
        load.wait()
    names = owner[...] == lax.broadcasted_iota(jnp.int32, (OWNERS, TILES), 0)
    mine = jnp.where(names, 1.0, 0.0).astype(BF16)
    onehot[...] = mine
    earlier = jnp.dot(mine, before[...], preferred_element_type=F32)
    earlier = jnp.where(names, earlier, 0.0).astype(BF16)
    slot = lax.dot_general(
        earlier, jnp.ones((OWNERS, 128), BF16), (((0,), (0,)), ((), ())), preferred_element_type=F32
    )
    lane_slot = (lax.broadcasted_iota(jnp.int32, (TILES, 128), 1) % 8).astype(F32)
    slotmask[...] = jnp.where(slot == lane_slot, 1.0, 0.0)

    sign_row = (1 - 2 * (row16 % 2)).astype(BF16)
    sign_part = jnp.where(lane16 < 64, 1.0, -1.0).astype(BF16)

    def samples_of(h, source):
        tiles = [zrcv[h, source, t] for t in range(3)] + [None] * 5
        plain, turned = [], []
        for tile in swap_pieces(tiles, (1, 2, 4)):
            tile = tile + pltpu.roll(tile, 32, 1) * sign_row
            plain.append(tile)
            turned.append(pltpu.roll(tile, 64, 1) * sign_part)
        return plain + turned

    def form(h):
        acc[...] = jnp.zeros_like(acc)

        @pl.loop(0, NZ // BATCH)
        def _(group):
            samples, waves = [], []
            for n in range(BATCH):
                source = rem(z + 16 - z_offset(group * BATCH + n), 16)
                pltpu.make_async_remote_copy(
                    zsnd.at[h, 0], zrcv.at[h, source], zsend.at[h], zrecv.at[h, source],
                    device_id=z_peer(1)[0], device_id_type=MESH,
                ).wait_recv()
            for n in range(BATCH):
                source = rem(z + 16 - z_offset(group * BATCH + n), 16)
                samples += samples_of(h, source)
                waves.append(tv[source])
            acc[...] += jnp.dot(
                jnp.concatenate(waves, axis=1), jnp.concatenate(samples, axis=0), preferred_element_type=F32
            )

        @pl.loop(0, ROWS // 64, unroll=4)
        def _(k):
            a = acc[pl.ds(pl.multiple_of(k * 64, 64), 64), :]
            b1 = pltpu.roll(a, 120, 1)
            b2 = pltpu.roll(a, 112, 1)
            others = (a, b1, b2, pltpu.roll(b1, 64, 1), pltpu.roll(b2, 64, 1))
            for n, other in enumerate(others):
                sums[pl.ds(pl.multiple_of(k * 8, 8), 8), n * 128 : (n + 1) * 128] = jnp.sum(
                    (a * other).reshape(8, 8, 128), axis=0
                )

        entries = sum(
            lax.dot_general(sel[...], part, (((1,), (1,)), ((), ())), preferred_element_type=F32)
            for part in split3(sums[...])
        )
        for turn in range(2):
            even, odd = entries[turn * 16 : turn * 16 + 8], entries[turn * 16 + 8 : turn * 16 + 16]
            scale = 1.0 / (odd[4:5] + EPSILON)
            even = even * scale
            odd = jnp.where(row8 == 4, odd, odd * scale)
            vout[h, 2 - 2 * turn] = jnp.where(lane8 < 64, even, pltpu.roll(odd, 64, 1))
            vout[h, 3 - 2 * turn] = jnp.where(lane8 < 64, pltpu.roll(even, 64, 1), odd)

    def gather(h, action):
        for g in range(NY):
            device = (x * 32 + (y * 4 + core * 2 + h) * 2 + z // 8, jnp.int32(g))
            here = (device[0] == pulse) & (y == g)
            source, target = vout.at[h, g], grcv.at[z % 8]

            @pl.when(jnp.logical_not(here))
            def _():
                copy = pltpu.make_async_remote_copy(
                    source, target, gsend, grecv, device_id=device, device_id_type=MESH
                )
                if action == "start":
                    copy.start()
                else:
                    copy.wait_send()

            if action == "start":

                @pl.when(here)
                def _():
                    pltpu.make_async_copy(source, target, grecv).start()

    for h in range(2):
        form(h)
        gather(h, "start")

    pltpu.make_async_remote_copy(grcv, grcv, gsend, grecv, device_id=plane_peer(1)[0], device_id_type=MESH).wait_recv()
    evens, odds = [], []
    for n in range(4):
        one, two = grcv[2 * n], grcv[2 * n + 1]
        evens.append(jnp.where(lane8 < 64, one, pltpu.roll(two, 64, 1)))
        odds.append(jnp.where(lane8 < 64, pltpu.roll(one, 64, 1), two))
    values = jnp.concatenate([jnp.concatenate(evens, axis=1), jnp.concatenate(odds, axis=1)], axis=0)
    wide = sum(
        lax.dot_general(part, spread[...], (((0,), (0,)), ((), ())), preferred_element_type=F32)
        for part in split3(values)
    )
    dealt = sum(
        jnp.dot(onehot[...], part, preferred_element_type=F32) for part in split3(wide * slotmask[...])
    )
    fsnd[...] = dealt.reshape(OWNERS, 1, 128)

    def place(p):
        return p % 16 * 8 + p // 16

    here = place(pulse)

    @pl.loop(1, OWNERS)
    def _(k):
        to = rem(pulse + k, OWNERS)
        pltpu.make_async_remote_copy(
            fsnd.at[to], frcv.at[here], fsend, frecv, device_id=(to, y), device_id_type=MESH
        ).start()

    frcv[here] = fsnd[pulse]
    final = pltpu.make_async_remote_copy(
        fsnd.at[pl.ds(0, OWNERS - 1)], frcv.at[pl.ds(0, OWNERS - 1)], fsend, frecv,
        device_id=plane_peer(1)[0], device_id_type=MESH,
    )
    for h in range(2):
        plane_all(h, PLANE - 1).wait_send()

        @pl.loop(1, NZ)
        def _(k):
            pltpu.make_async_remote_copy(
                zsnd.at[h, 0], zrcv.at[h, 0], zsend.at[h], zrecv.at[h, 0],
                device_id=z_peer(1)[0], device_id_type=MESH,
            ).wait_send()

        gather(h, "wait")
    final.wait_recv()
    arrived = frcv[...].reshape(OWNERS, 128)
    parts = split3(arrived)
    row = lax.broadcasted_iota(jnp.int32, (OWNERS, 128), 0)
    lane = lax.broadcasted_iota(jnp.int32, (OWNERS, 128), 1)
    own_lane = row // 8 == lane // 8
    for v in range(10):
        wide = sum(
            jnp.dot(part, pick[:, v * 128 : (v + 1) * 128], preferred_element_type=F32) for part in parts
        )
        out[v] = jnp.sum(jnp.where(own_lane, wide, 0.0).reshape(16, 8, 128), axis=0)

    final.wait_send()


def on_device(echoes, interp_weights, band_starts, row_lo, row_len, tile_owner):
    vmem = pl.BlockSpec(memory_space=pltpu.VMEM)
    hbm = pl.BlockSpec(memory_space=pl.ANY)
    sel, before, spread, pick = selectors()
    dma = pltpu.SemaphoreType.DMA
    annulus = resample(echoes.reshape(2, 16, 8192), interp_weights, band_starts, row_lo, row_len)
    moments = pl.pallas_call(
        body,
        out_shape=jax.ShapeDtypeStruct((10, 8, 128), F32),
        in_specs=[hbm] * 7,
        out_specs=vmem,
        scratch_shapes=[
            pltpu.VMEM((1, TILES), jnp.int32),
            pltpu.VMEM((NZ, ROWS, 256), BF16),
            pltpu.VMEM((32, 640), BF16),
            pltpu.VMEM((TILES, TILES), BF16),
            pltpu.VMEM((16, 128), BF16),
            pltpu.VMEM((128, 1280), BF16),
            pltpu.VMEM((2, PLANE, 2, 16, 128), BF16),
            pltpu.VMEM((2, NZ, 3, 16, 128), BF16),
            pltpu.VMEM((2, NZ, 3, 16, 128), BF16),
            pltpu.VMEM((ROWS, 128), F32),
            pltpu.VMEM((128, 640), F32),
            pltpu.VMEM((2, NY, 8, 128), F32),
            pltpu.VMEM((8, 8, 128), F32),
            pltpu.VMEM((OWNERS, TILES), BF16),
            pltpu.VMEM((TILES, 128), F32),
            pltpu.VMEM((OWNERS, 1, 128), F32),
            pltpu.VMEM((OWNERS, 1, 128), F32),
            dma((6,)), dma((2,)), dma((2,)), dma((2,)), dma((2, NZ)), dma, dma, dma, dma,
        ],
        compiler_params=pltpu.CompilerParams(
            collective_id=0, has_side_effects=True, vmem_limit_bytes=VMEM_LIMIT
        ),
    )(
        annulus,
        tile_owner.reshape(1, TILES),
        jnp.asarray(tables()),
        *[jnp.asarray(a) for a in (sel, before, spread, pick)],
    )
    return moments.reshape(10, 1, 1, 1024)


def solution(mesh):
    return jax.shard_map(
        on_device,
        mesh=mesh,
        in_specs=(
            P(None, "pol", "pulse", None),
            P(),
            P(),
            P("pulse"),
            P("pulse"),
            P("pol", "pulse", None, None),
        ),
        out_specs=P(None, "pol", "pulse", None),
        check_vma=False,
    )
```
